32 devices in a mesh: attn: 4 (over z), expert: 8 (over y, x, core).
Axes of the slice: x: 2, y: 2, z: 4, core: 2. Of those that a mesh axis runs over, the one named last changes fastest.
Arguments:
- tokens: bfloat16 [8, 512, 2048], P('expert', 'attn'), may hold values from -3 to 5
- lengths: int32 [8, 3], P('expert'), may hold values from 1 to 384, 512 in all within a row
- page_table: int32 [8, 3, 4], P('expert'), may hold values from 0 to 11, as said below
- routes: int32 [8, 512, 6], P('expert'), may hold values from 0 to 63, all different within a row; in each aligned block of 512 rows (0 to 511, 512 to 1023, ..., all dimensions but the last counted through in order) at most 56 rows name the same one
- attn_gain: bfloat16 [2048], replicated, may hold values from 0.099609375 to 1.8984375
- w_query: bfloat16 [2048, 3072], P(None, 'attn'), may hold values from -0.125 to 0.125
- w_latent: bfloat16 [2048, 576], replicated, may hold values from -0.125 to 0.125
- latent_gain: bfloat16 [512], replicated, may hold values from 0.099609375 to 1.8984375
- w_key: bfloat16 [512, 2048], P(None, 'attn'), may hold values from -0.25 to 0.25
- w_value: bfloat16 [512, 2048], P(None, 'attn'), may hold values from -0.25 to 0.25
- w_out: bfloat16 [2048, 2048], P('attn'), may hold values from -0.125 to 0.125
- ffn_gain: bfloat16 [2048], replicated, may hold values from 0.099609375 to 1.8984375
- w_router: bfloat16 [2048, 64], replicated, may hold values from -0.08985319 to 0.08985319
- expert_gate: bfloat16 [64, 2048, 1408], P('expert', None, 'attn'), may hold values from -0.375 to 0.375
- expert_up: bfloat16 [64, 2048, 1408], P('expert', None, 'attn'), may hold values from -0.375 to 0.375
- expert_down: bfloat16 [64, 1408, 2048], P('expert', 'attn'), may hold values from -7.462025 to 7.462025
- shared_gate: bfloat16 [2048, 1408], P(None, 'attn'), may hold values from -0.125 to 0.125
- shared_up: bfloat16 [2048, 1408], P(None, 'attn'), may hold values from -0.125 to 0.125
- shared_down: bfloat16 [1408, 2048], P('attn'), may hold values from -0.15625 to 0.15625
Outputs:
- layer_out: bfloat16 [8, 512, 2048], P('expert', 'attn')
- latent_pages: bfloat16 [8, 12, 128, 512], P('expert', 'attn')
- rope_pages: bfloat16 [8, 12, 64, 128], P('expert', 'attn')
The draws below stay inside these ranges and needn't reach their ends.
Inputs may be any that keep to these rules, and one draw needn't show every extreme that they name: `page_table`: each group's table holds every slot 0 to 11 exactly once; entries past a prompt's last page are unused. The 3 lengths of a group sum to 512 and the longest is exactly 384. `routes`: a row names 6 different experts; within one group's 512 rows no expert is named more than 56 times, a bound that some block reaches.
All inputs are finite; a program needn't handle non-finite values.
Results may differ from the reference program's by a relative error of at most 0.029.
Values may be sent and summed in bfloat16 or wider, within the bound.
A program may use at most 192 MiB of HBM per device.

```python
import math
import jax
import jax.numpy as jnp
import numpy as np
from jax import lax

D = 2048
HEADS = 16
NOPE = 128
ROPE = 64
VDIM = 128
LAT = 512
EXPERTS = 64
TOP = 6
FFE = 1408
FFS = 1408
PAGE = 128
SEGS = 3
GROUPS = 8
G = 512
MOST_LEN = 384
MAXPG = 4
SLOTS = 12
CAP = 56
N_ATTN = 4


def draw_page_table(key, part):
    group_keys = jax.random.split(key, GROUPS)

    def one_table(group_key):
        return jax.random.permutation(group_key, SLOTS)
    tables = jax.vmap(one_table)(group_keys)
    return tables.reshape(GROUPS, SEGS, MAXPG).astype(jnp.int32)


def router_levels(key):
    return jax.random.uniform(jax.random.fold_in(key, 7), (EXPERTS,), jnp.float32, -2.6, 2.6)


def draw_tokens(key, part):
    token_key = jax.random.fold_in(key, 21)
    noise = jnp.clip(jax.random.normal(token_key, (GROUPS, G, D), jnp.float32), -6.0, 6.0)
    values = 0.6 * noise + 0.8
    return values.astype(jnp.bfloat16)


def draw_w_router(key, part):
    noise_key = jax.random.fold_in(key, 11)
    noise = jnp.clip(jax.random.normal(noise_key, (D, EXPERTS), jnp.float32), -6.0, 6.0)
    levels = router_levels(key)
    values = 0.6 * noise * D ** (-0.5) + levels[None, :] * (1.0 / D)
    return values.astype(jnp.bfloat16)


def draw_expert_down(key, part):
    noise_key = jax.random.fold_in(key, 13)
    noise = jnp.clip(jax.random.normal(noise_key, (EXPERTS, FFE, D), jnp.float32), -6.0, 6.0)
    levels = router_levels(key)
    scales = 6.4 * jnp.exp(-0.76 * levels)
    values = noise * scales[:, None, None] * FFE ** (-0.5)
    return values.astype(jnp.bfloat16)


def block_levels(rng, extent, shards, smallest, top_value):
    factor_of, own = 1.0, jax.random.fold_in(rng, 6)
    for dim, parts in shards:
        steps = jnp.exp(jax.random.uniform(jax.random.fold_in(own, dim), (parts,), jnp.float32, smallest / len(shards), top_value / len(shards)))
        factor_of = factor_of * jnp.repeat(steps, extent[dim] // parts).reshape([-1 if axis == dim else 1 for axis in range(len(extent))])
    return factor_of


def profile(amount, total, reach, lean):
    weights = [(1 << 20) // math.isqrt(rank ** lean) + 1 for rank in range(2, amount + 1)]
    rest, counts = total - reach - (amount - 1), [1] * (amount - 1)
    while rest > 0:
        movable = [i for i in range(amount - 1) if counts[i] < reach]
        pool, budget = sum([weights[i] for i in movable]), rest
        for i in movable:
            more = min(reach - counts[i], max(1, budget * weights[i] // pool), rest)
            counts[i] = counts[i] + more
            rest = rest - more
    return np.array([reach] + counts)


def uneven_parts(rng, count, total, most, skew):
    if count == 2:
        one = jax.random.randint(rng, (), max(1, total - most), min(most, total - 1) + 1)
        return jnp.stack([one, total - one])
    sizes = jnp.asarray(profile(count, total, most, skew), jnp.int32)
    pairs = (count - 1) // 2
    donor, taker = sizes[1:1 + 2 * pairs:2], sizes[2:2 + 2 * pairs:2]
    margin = jnp.minimum(donor - 1, most - taker)
    passed = jax.random.randint(jax.random.fold_in(rng, 1), (pairs,), 0, 1 << 20) % (margin + 1)
    sizes = sizes.at[1:1 + 2 * pairs:2].set(donor - passed).at[2:2 + 2 * pairs:2].set(taker + passed)
    return sizes[jax.random.permutation(jax.random.fold_in(rng, 2), count)]


def routed_block(key, own, number, rows, number_of, top, most, skew):
    order = jax.random.permutation(key, number_of)
    packed, usual = portions_of(number_of, rows * top, most, skew, True), portions_of(number_of, rows * top, most, skew, False)
    places = jnp.arange(number_of)

    def named(tallies, turn):
        used = int((tallies > 0).sum())
        fixed = max(1, used // 4)
        passed = fixed + (places - fixed + turn * (used - fixed)) % max(1, number_of - fixed)
        return jnp.zeros((number_of,), jnp.int32).at[order[jnp.where(places < fixed, places, passed)]].set(jnp.asarray(tallies, jnp.int32))

    tallies = jnp.where(number % 4 == 0, named(packed, number // 4), named(usual, number - number // 4 - 1))
    mixed = jax.random.permutation(jax.random.fold_in(own, 3), number_of)
    giver, receiver = mixed[0:number_of // 2 * 2:2], mixed[1:number_of // 2 * 2:2]
    room = jnp.minimum(tallies[giver] - 1, most - tallies[receiver]) // 2
    room = jnp.where((giver == order[0]) | (receiver == order[0]) | (tallies[receiver] == 0), 0, jnp.maximum(room, 0))
    passed = jax.random.randint(jax.random.fold_in(own, 4), (number_of // 2,), 0, 1 << 20) % (room + 1)
    tallies = tallies.at[giver].add(-passed).at[receiver].add(passed)
    items = jnp.searchsorted(jnp.cumsum(tallies), jnp.arange(rows * top), side="right").astype(jnp.int32)
    table = items.reshape(top, rows).T
    table = table[jax.random.permutation(jax.random.fold_in(own, 1), rows)]
    turn = jax.random.randint(jax.random.fold_in(own, 2), (rows, 1), 0, top)
    return jnp.take_along_axis(table, (jnp.arange(top)[None, :] + turn) % top, axis=1)


def portions_of(amount, total, limit, slope, full):
    weights = [(1 << 20) // math.isqrt(rank ** slope) + 1 for rank in range(1, amount + 1)]
    largest = limit if full else min(limit, max(-(-total // amount), total * weights[0] // sum(weights)))
    least = 1 if total - largest >= amount - 1 else 0
    given, spare = [largest] + [least] * (amount - 1), total - largest - least * (amount - 1)
    while spare > 0:
        free = [i for i in range(1, amount) if given[i] < largest] or [i for i in range(1, amount) if given[i] < limit]
        pool, left = sum([weights[i] for i in free]), spare
        for i in free:
            extra = min(limit - given[i], max(1, left * weights[i] // pool), spare)
            given[i] = given[i] + extra
            spare = spare - extra
    return np.array(given)


def normal_values(stream_key, dims, width, limit, cuts=(), held_as=jnp.bfloat16):
    level = block_levels(stream_key, dims, cuts, -0.22, 0.18) if cuts else 1.0
    values = jax.random.normal(stream_key, dims, jnp.float32) * width * level
    return jnp.minimum(jnp.maximum(values, -limit), limit).astype(held_as)


def setup_inputs(seed: int = 0) -> dict:
    streams_of = jax.random.split(jax.random.key(seed), 20)
    tokens = draw_tokens(jax.random.fold_in(streams_of[19], 71), 0)
    lengths = jax.vmap(lambda own: uneven_parts(own, SEGS, G, MOST_LEN, 2))(jax.random.split(streams_of[1], GROUPS)).reshape((GROUPS, SEGS)).astype(jnp.int32)
    page_table = draw_page_table(jax.random.fold_in(streams_of[19], 71), 0)
    routes_keys = jax.random.split(jax.random.fold_in(streams_of[3], 1), GROUPS * G // G)
    routes_turns = jax.random.permutation(jax.random.fold_in(streams_of[3], 3), GROUPS * G // G)
    routes = jax.vmap(lambda own, number: routed_block(jax.random.fold_in(streams_of[3], 2), own, number, G, EXPERTS, TOP, CAP, 1))(routes_keys, routes_turns).reshape((GROUPS, G, TOP))
    attn_gain = jnp.clip(1.0 + 0.18 * jax.random.normal(streams_of[4], (D,), jnp.float32), 0.099609375, 1.8984375).astype(jnp.bfloat16)
    w_query = normal_values(streams_of[5], (D, HEADS * (NOPE + ROPE)), D ** -0.5, 0.125, ((1, 4),))
    w_latent = normal_values(streams_of[6], (D, LAT + ROPE), D ** -0.5, 0.125)
    latent_gain = jnp.clip(1.0 + 0.18 * jax.random.normal(streams_of[7], (LAT,), jnp.float32), 0.099609375, 1.8984375).astype(jnp.bfloat16)
    w_key = normal_values(streams_of[8], (LAT, HEADS * NOPE), LAT ** -0.5, 0.25, ((1, 4),))
    w_value = normal_values(streams_of[9], (LAT, HEADS * VDIM), LAT ** -0.5, 0.25, ((1, 4),))
    w_out = normal_values(streams_of[10], (HEADS * VDIM, D), (HEADS * VDIM) ** -0.5, 0.125, ((0, 4),))
    ffn_gain = jnp.clip(1.0 + 0.18 * jax.random.normal(streams_of[11], (D,), jnp.float32), 0.099609375, 1.8984375).astype(jnp.bfloat16)
    w_router = draw_w_router(jax.random.fold_in(streams_of[19], 71), 0)
    expert_gate = normal_values(streams_of[13], (EXPERTS, D, FFE), (D // 8) ** -0.5, 0.375, ((0, 8), (2, 4)))
    expert_up = normal_values(streams_of[14], (EXPERTS, D, FFE), (D // 8) ** -0.5, 0.375, ((0, 8), (2, 4)))
    expert_down = draw_expert_down(jax.random.fold_in(streams_of[19], 71), 0)
    shared_gate = normal_values(streams_of[16], (D, FFS), D ** -0.5, 0.125, ((1, 4),))
    shared_up = normal_values(streams_of[17], (D, FFS), D ** -0.5, 0.125, ((1, 4),))
    shared_down = normal_values(streams_of[18], (FFS, D), FFS ** -0.5, 0.15625, ((0, 4),))
    return {"tokens": tokens, "lengths": lengths, "page_table": page_table, "routes": routes, "attn_gain": attn_gain, "w_query": w_query, "w_latent": w_latent, "latent_gain": latent_gain, "w_key": w_key, "w_value": w_value, "w_out": w_out, "ffn_gain": ffn_gain, "w_router": w_router, "expert_gate": expert_gate, "expert_up": expert_up, "expert_down": expert_down, "shared_gate": shared_gate, "shared_up": shared_up, "shared_down": shared_down}


epsilon = 1e-06

def rms_apply(values, gain_vec):
    mean_square = lax.optimization_barrier(jnp.mean(values * values, axis=-1, keepdims=True))
    return values * lax.rsqrt(mean_square + epsilon) * gain_vec.astype(jnp.float32)

def rope_tables(positions, width_rope):
    half_width = width_rope // 2
    freq_index = jnp.arange(half_width, dtype=jnp.float32)
    inverse_freq = jnp.exp(freq_index * (-2.0 * math.log(10000.0) / width_rope))
    angles = positions.astype(jnp.float32)[:, None] * inverse_freq[None, :]
    return (jnp.cos(angles), jnp.sin(angles))

def rope_apply(values, cosine, sine):
    half_width = values.shape[-1] // 2
    first_half = values[..., :half_width]
    second_half = values[..., half_width:]
    return jnp.concatenate([first_half * cosine - second_half * sine, second_half * cosine + first_half * sine], axis=-1)

def segment_info(seg_lengths, group_rows):
    ends = jnp.cumsum(seg_lengths).astype(jnp.int32)
    starts = (ends - seg_lengths).astype(jnp.int32)
    row_ids = jnp.arange(group_rows, dtype=jnp.int32)
    seg_of_row = lax.optimization_barrier(jnp.sum((row_ids[:, None] >= ends[None, :]).astype(jnp.int32), axis=1)).astype(jnp.int32)
    seg_match = seg_of_row[:, None] == jnp.arange(seg_lengths.shape[0], dtype=jnp.int32)[None, :]
    positions = (row_ids - lax.optimization_barrier(jnp.sum(jnp.where(seg_match, starts[None, :], 0), axis=1))).astype(jnp.int32)
    return (starts, seg_of_row, positions, row_ids)

def write_pages(latent, key_rope, seg_lengths, starts, table, slot_ids, page_len):
    seg_count = table.shape[0]
    pages_per = table.shape[1]
    match = table[None, :, :] == slot_ids[:, None, None]
    seg_pick = lax.optimization_barrier(jnp.sum(jnp.where(match, jnp.arange(seg_count, dtype=jnp.int32)[None, :, None], 0), axis=(1, 2))).astype(jnp.int32)
    page_pick = lax.optimization_barrier(jnp.sum(jnp.where(match, jnp.arange(pages_per, dtype=jnp.int32)[None, None, :], 0), axis=(1, 2))).astype(jnp.int32)
    seg_match = seg_pick[:, None] == jnp.arange(seg_count, dtype=jnp.int32)[None, :]
    first_row = lax.optimization_barrier(jnp.sum(jnp.where(seg_match, starts[None, :], 0), axis=1)).astype(jnp.int32)
    seg_len = lax.optimization_barrier(jnp.sum(jnp.where(seg_match, seg_lengths[None, :], 0), axis=1)).astype(jnp.int32)
    offsets = page_pick[:, None] * page_len + jnp.arange(page_len, dtype=jnp.int32)[None, :]
    valid = offsets < seg_len[:, None]
    row_index = jnp.minimum(first_row[:, None] + offsets, latent.shape[0] - 1).astype(jnp.int32)
    latent_rows = jnp.take(latent, row_index, axis=0)
    rope_rows = jnp.take(key_rope, row_index, axis=0)
    zero_value = jnp.zeros((), latent.dtype)
    latent_out = jnp.where(valid[:, :, None], latent_rows, zero_value)
    rope_out = jnp.where(valid[:, None, :], jnp.transpose(rope_rows, (0, 2, 1)), zero_value)
    return (latent_out, rope_out)

def reference(tokens, lengths, page_table, routes, attn_gain, w_query, w_latent, latent_gain, w_key, w_value, w_out, ffn_gain, w_router, expert_gate, expert_up, expert_down, shared_gate, shared_up, shared_down):
    score_scale = (NOPE + ROPE) ** (-0.5)

    def group_attention(group_args):
        tokens_group, seg_lengths, table = group_args
        group_rows = tokens_group.shape[0]
        starts, seg_of_row, positions, row_ids = segment_info(seg_lengths, group_rows)
        residual = tokens_group.astype(jnp.float32)
        normed = rms_apply(residual, attn_gain).astype(jnp.bfloat16)
        query_raw = jnp.dot(normed, w_query, preferred_element_type=jnp.float32).reshape(group_rows, HEADS, NOPE + ROPE)
        compressed = jnp.dot(normed, w_latent, preferred_element_type=jnp.float32)
        cosine, sine = rope_tables(positions, ROPE)
        query_all = jnp.concatenate([query_raw[..., :NOPE], rope_apply(query_raw[..., NOPE:], cosine[:, None, :], sine[:, None, :])], axis=-1).astype(jnp.bfloat16)
        latent = rms_apply(compressed[:, :LAT], latent_gain).astype(jnp.bfloat16)
        key_rope = rope_apply(compressed[:, LAT:], cosine, sine).astype(jnp.bfloat16)
        key_nope = jnp.dot(latent, w_key, preferred_element_type=jnp.float32).astype(jnp.bfloat16).reshape(group_rows, HEADS, NOPE)
        value_rows = jnp.dot(latent, w_value, preferred_element_type=jnp.float32).astype(jnp.bfloat16).reshape(group_rows, HEADS, VDIM)
        score_nope = jnp.einsum('qhd,khd->hqk', query_all[..., :NOPE].astype(jnp.float32), key_nope.astype(jnp.float32))
        score_rope = jnp.einsum('qhd,kd->hqk', query_all[..., NOPE:].astype(jnp.float32), key_rope.astype(jnp.float32))
        scores = (score_nope + score_rope) * score_scale
        allowed = (seg_of_row[:, None] == seg_of_row[None, :]) & (row_ids[None, :] <= row_ids[:, None])
        weights = jnp.where(allowed[None, :, :], jnp.exp(scores), 0.0)
        probs = (weights / lax.optimization_barrier(jnp.sum(weights, axis=-1, keepdims=True))).astype(jnp.bfloat16)
        mixed = jnp.einsum('hqk,khd->qhd', probs.astype(jnp.float32), value_rows.astype(jnp.float32)).astype(jnp.bfloat16).reshape(group_rows, HEADS * VDIM)
        hidden = residual + jnp.dot(mixed, w_out, preferred_element_type=jnp.float32)
        slot_ids = jnp.arange(SLOTS, dtype=jnp.int32)
        latent_out, rope_out = write_pages(latent, key_rope, seg_lengths, starts, table, slot_ids, PAGE)
        return (hidden, latent_out, rope_out)
    hidden_all, latent_pages, rope_pages = lax.map(group_attention, (tokens, lengths, page_table))
    total_rows = GROUPS * G
    flat_hidden = hidden_all.reshape(total_rows, D)
    normed_ffn = rms_apply(flat_hidden, ffn_gain).astype(jnp.bfloat16)
    logits = jnp.dot(normed_ffn, w_router, preferred_element_type=jnp.float32)
    exp_logits = jnp.exp(logits)
    router = exp_logits / lax.optimization_barrier(jnp.sum(exp_logits, axis=1, keepdims=True))
    route_flat = routes.reshape(total_rows, TOP)
    expert_ids = jnp.arange(EXPERTS, dtype=jnp.int32)
    route_hits = route_flat[:, :, None] == expert_ids[None, None, :]
    pair_weight = lax.optimization_barrier(jnp.sum(jnp.where(route_hits, router[:, None, :], 0.0), axis=2))
    group_hits = route_hits.reshape(GROUPS, G * TOP, EXPERTS).astype(jnp.int32)
    slot_of_pair = (lax.optimization_barrier(jnp.sum(jnp.cumsum(group_hits, axis=1).astype(jnp.int32) * group_hits, axis=2)) - 1).astype(jnp.int32)
    group_ids = jnp.arange(GROUPS, dtype=jnp.int32)[:, None]
    column = (group_ids * CAP + slot_of_pair).reshape(-1).astype(jnp.int32)
    pair_expert = route_flat.reshape(-1).astype(jnp.int32)
    pair_rows = jnp.repeat(jnp.arange(total_rows, dtype=jnp.int32), TOP).astype(jnp.int32)
    sources = jnp.full((EXPERTS, GROUPS * CAP), total_rows, jnp.int32).at[pair_expert, column].set(pair_rows)
    slot_weight = jnp.zeros((EXPERTS, GROUPS * CAP), jnp.float32).at[pair_expert, column].set(pair_weight.reshape(-1))
    padded_rows = jnp.concatenate([normed_ffn, jnp.zeros((1, D), jnp.bfloat16)], axis=0)
    quarter = FFE // N_ATTN

    def expert_step(accum, expert_args):
        gate_w, up_w, down_w, source_ids, scale_ids = expert_args
        picked = jnp.take(padded_rows, source_ids, axis=0)
        gate_act = jnp.dot(picked, gate_w, preferred_element_type=jnp.float32)
        up_act = jnp.dot(picked, up_w, preferred_element_type=jnp.float32)
        hidden_act = (jax.nn.silu(gate_act) * up_act).astype(jnp.bfloat16)
        partial_total = jnp.zeros((picked.shape[0], D), jnp.float32)
        for index in range(N_ATTN):
            part_value = jnp.dot(hidden_act[:, index * quarter:(index + 1) * quarter], down_w[index * quarter:(index + 1) * quarter], preferred_element_type=jnp.float32).astype(jnp.bfloat16)
            part_value = lax.optimization_barrier(part_value)
            partial_total = partial_total + part_value.astype(jnp.float32)
        return (accum.at[source_ids].add(scale_ids[:, None] * partial_total), None)
    accum_init = jnp.zeros((total_rows + 1, D), jnp.float32)
    accum_done, _ = lax.scan(expert_step, accum_init, (expert_gate, expert_up, expert_down, sources, slot_weight))
    routed = accum_done[:total_rows]
    shared_hidden = (jax.nn.silu(jnp.dot(normed_ffn, shared_gate, preferred_element_type=jnp.float32)) * jnp.dot(normed_ffn, shared_up, preferred_element_type=jnp.float32)).astype(jnp.bfloat16)
    shared_out = jnp.dot(shared_hidden, shared_down, preferred_element_type=jnp.float32)
    layer_out = (flat_hidden + routed + shared_out).astype(jnp.bfloat16).reshape(GROUPS, G, D)
    return (layer_out, latent_pages, rope_pages)
```

```python
import math

import jax
import jax.numpy as jnp
from jax import lax
from jax.sharding import PartitionSpec as P

NOPE = 128
ROPE = 64
VDIM = 128
LAT = 512
EXPERTS = 64
TOP = 6
PAGE = 128


epsilon = 1e-06


def rms_apply(values, gain_vec):
    mean_square = jnp.mean(values * values, axis=-1, keepdims=True)
    return values * lax.rsqrt(mean_square + epsilon) * gain_vec.astype(jnp.float32)


def rope_tables(positions, width_rope):
    half_width = width_rope // 2
    freq_index = jnp.arange(half_width, dtype=jnp.float32)
    inverse_freq = jnp.exp(freq_index * (-2.0 * math.log(10000.0) / width_rope))
    angles = positions.astype(jnp.float32)[:, None] * inverse_freq[None, :]
    return (jnp.cos(angles), jnp.sin(angles))


def rope_apply(values, cosine, sine):
    half_width = values.shape[-1] // 2
    first_half = values[..., :half_width]
    second_half = values[..., half_width:]
    return jnp.concatenate(
        [first_half * cosine - second_half * sine, second_half * cosine + first_half * sine],
        axis=-1,
    )


def write_pages(latent, key_rope, seg_lengths, starts, table, slot_ids, page_len):
    seg_count = table.shape[0]
    pages_per = table.shape[1]
    match = table[None, :, :] == slot_ids[:, None, None]
    seg_pick = jnp.sum(
        jnp.where(match, jnp.arange(seg_count, dtype=jnp.int32)[None, :, None], 0), axis=(1, 2)
    )
    page_pick = jnp.sum(
        jnp.where(match, jnp.arange(pages_per, dtype=jnp.int32)[None, None, :], 0), axis=(1, 2)
    )
    seg_match = seg_pick[:, None] == jnp.arange(seg_count, dtype=jnp.int32)[None, :]
    first_row = jnp.sum(jnp.where(seg_match, starts[None, :], 0), axis=1)
    seg_len = jnp.sum(jnp.where(seg_match, seg_lengths[None, :], 0), axis=1)
    offsets = page_pick[:, None] * page_len + jnp.arange(page_len, dtype=jnp.int32)[None, :]
    valid = offsets < seg_len[:, None]
    row_index = jnp.minimum(first_row[:, None] + offsets, latent.shape[0] - 1)
    latent_rows = jnp.take(latent, row_index, axis=0)
    rope_rows = jnp.take(key_rope, row_index, axis=0)
    zero_value = jnp.zeros((), latent.dtype)
    latent_out = jnp.where(valid[:, :, None], latent_rows, zero_value)
    rope_out = jnp.where(valid[:, None, :], jnp.transpose(rope_rows, (0, 2, 1)), zero_value)
    return (latent_out, rope_out)


def pick_matrix(routes_all, first_expert, local_experts, capacity):
    ids = first_expert + jnp.arange(local_experts, dtype=jnp.int32)
    hits = jnp.any(routes_all[:, None, :, :] == ids[None, :, None, None], axis=3)
    row_ids = jnp.arange(hits.shape[2], dtype=jnp.int32)
    earlier = (row_ids[:, None] < row_ids[None, :]).astype(jnp.bfloat16)
    before = jnp.einsum(
        "gek,kr->ger", hits.astype(jnp.bfloat16), earlier, preferred_element_type=jnp.float32
    ).astype(jnp.int32)
    slots = jnp.where(hits, before, -1)
    wanted = jnp.arange(capacity, dtype=jnp.int32)
    return (slots[:, :, None, :] == wanted[None, None, :, None]).astype(jnp.bfloat16)


def local(
    tokens,
    lengths,
    page_table,
    routes,
    attn_gain,
    w_query,
    w_latent,
    latent_gain,
    w_key,
    w_value,
    w_out,
    ffn_gain,
    w_router,
    expert_gate,
    expert_up,
    expert_down,
    shared_gate,
    shared_up,
    shared_down,
):
    quarters = lax.axis_size("attn")
    rank_attn = lax.axis_index("attn")
    owners = lax.axis_size("expert")
    own_rows = tokens.shape[1]
    group_rows = own_rows * quarters
    heads_here = w_value.shape[1] // VDIM
    local_experts = expert_gate.shape[0]
    capacity = quarters * (
        (7 * group_rows * TOP + 6 * EXPERTS * quarters - 1) // (6 * EXPERTS * quarters)
    )
    score_scale = (NOPE + ROPE) ** (-0.5)
    routes_all = lax.all_gather(routes[0], "expert", axis=0)
    first_expert = lax.axis_index("expert") * local_experts
    residual_own = tokens[0].astype(jnp.float32)
    normed_own = rms_apply(residual_own, attn_gain).astype(jnp.bfloat16)
    piece = lax.all_gather(normed_own, "attn", axis=0, tiled=True)
    projected = jnp.concatenate(
        [
            jnp.dot(piece, w_query, preferred_element_type=jnp.float32),
            jnp.dot(piece, w_latent, preferred_element_type=jnp.float32),
        ],
        axis=1,
    )
    seg_lengths = lengths[0]
    seg_ids = jnp.arange(seg_lengths.shape[0], dtype=jnp.int32)
    ends = jnp.sum(
        jnp.where(seg_ids[None, :] <= seg_ids[:, None], seg_lengths[None, :], 0), axis=1
    )
    starts = ends - seg_lengths
    row_ids = jnp.arange(group_rows, dtype=jnp.int32)
    seg_of_row = jnp.sum((row_ids[:, None] >= ends[None, :]).astype(jnp.int32), axis=1)
    seg_match = seg_of_row[:, None] == jnp.arange(seg_lengths.shape[0], dtype=jnp.int32)[None, :]
    positions = row_ids - jnp.sum(jnp.where(seg_match, starts[None, :], 0), axis=1)
    cosine, sine = rope_tables(positions, ROPE)
    query_width = w_query.shape[1]
    query_raw = projected[:, :query_width].reshape(group_rows, heads_here, NOPE + ROPE)
    query_all = jnp.concatenate(
        [
            query_raw[..., :NOPE],
            rope_apply(query_raw[..., NOPE:], cosine[:, None, :], sine[:, None, :]),
        ],
        axis=-1,
    ).astype(jnp.bfloat16)
    compressed = projected[:, query_width:]
    latent = rms_apply(compressed[:, :LAT], latent_gain).astype(jnp.bfloat16)
    key_rope = rope_apply(compressed[:, LAT:], cosine, sine).astype(jnp.bfloat16)
    key_nope = (
        jnp.dot(latent, w_key, preferred_element_type=jnp.float32)
        .astype(jnp.bfloat16)
        .reshape(group_rows, heads_here, NOPE)
    )
    value_rows = (
        jnp.dot(latent, w_value, preferred_element_type=jnp.float32)
        .astype(jnp.bfloat16)
        .reshape(group_rows, heads_here, VDIM)
    )
    slots_here = page_table.shape[1] * page_table.shape[2] // quarters
    slot_ids = rank_attn * slots_here + jnp.arange(slots_here, dtype=jnp.int32)
    latent_out, rope_out = write_pages(
        latent, key_rope, seg_lengths, starts, page_table[0], slot_ids, PAGE
    )
    query_ids = jnp.arange(group_rows, dtype=jnp.int32)
    score_nope = jnp.einsum(
        "qhd,khd->hqk", query_all[..., :NOPE], key_nope, preferred_element_type=jnp.float32
    )
    score_rope = jnp.einsum(
        "qhd,kd->hqk", query_all[..., NOPE:], key_rope, preferred_element_type=jnp.float32
    )
    scores = (score_nope + score_rope) * score_scale
    allowed = (seg_of_row[:, None] == seg_of_row[None, :]) & (
        row_ids[None, :] <= query_ids[:, None]
    )
    weights = jnp.where(allowed[None, :, :], jnp.exp(scores), 0.0)
    probs = (weights / jnp.sum(weights, axis=-1, keepdims=True)).astype(jnp.bfloat16)
    mixed = (
        jnp.einsum("hqk,khd->qhd", probs, value_rows, preferred_element_type=jnp.float32)
        .astype(jnp.bfloat16)
        .reshape(group_rows, heads_here * VDIM)
    )
    term_all = jnp.dot(mixed, w_out, preferred_element_type=jnp.float32)
    attn_own = lax.psum_scatter(
        term_all.astype(jnp.bfloat16), "attn", scatter_dimension=0, tiled=True
    ).astype(jnp.float32)
    hidden_own = residual_own + attn_own
    normed_ffn = rms_apply(hidden_own, ffn_gain).astype(jnp.bfloat16)
    normed_all = lax.all_gather(normed_ffn, "attn", axis=0, tiled=True)
    rows_all = lax.all_gather(normed_all, "expert", axis=0)
    width = normed_all.shape[1]

    picks = pick_matrix(routes_all, first_expert, local_experts, capacity)

    logits = jnp.einsum("grd,dx->grx", rows_all, w_router, preferred_element_type=jnp.float32)
    exp_logits = jnp.exp(logits)
    router = exp_logits / jnp.sum(exp_logits, axis=-1, keepdims=True)
    router_here = lax.dynamic_slice_in_dim(router, first_expert, local_experts, 2)
    here = jnp.transpose(router_here, (2, 0, 1))
    slot_weight = jnp.sum(
        jnp.where(jnp.transpose(picks, (1, 0, 2, 3)) > 0, here[:, :, None, :], 0.0), axis=3
    ).reshape(local_experts, owners * capacity, 1)
    arrived = (
        jnp.einsum("gesr,grd->egsd", picks, rows_all, preferred_element_type=jnp.float32)
        .astype(jnp.bfloat16)
        .reshape(local_experts, owners * capacity, width)
    )
    gate_act = jnp.einsum("ech,ehf->ecf", arrived, expert_gate, preferred_element_type=jnp.float32)
    up_act = jnp.einsum("ech,ehf->ecf", arrived, expert_up, preferred_element_type=jnp.float32)
    hidden_act = (jax.nn.silu(gate_act) * up_act * slot_weight).astype(jnp.bfloat16)
    worked = (
        jnp.einsum("ecf,efh->ech", hidden_act, expert_down, preferred_element_type=jnp.float32)
        .astype(jnp.bfloat16)
        .reshape(local_experts, owners, capacity, width)
    )
    shared_hidden = (
        jax.nn.silu(jnp.dot(normed_all, shared_gate, preferred_element_type=jnp.float32))
        * jnp.dot(normed_all, shared_up, preferred_element_type=jnp.float32)
    ).astype(jnp.bfloat16)
    shared_term = jnp.dot(shared_hidden, shared_down, preferred_element_type=jnp.float32)
    partial = jnp.einsum(
        "gesr,egsd->grd", picks, worked, preferred_element_type=jnp.float32
    ).astype(jnp.bfloat16)
    group_sum = lax.psum_scatter(partial, "expert", scatter_dimension=0, tiled=False)
    ffn_term = (group_sum.astype(jnp.float32) + shared_term).astype(jnp.bfloat16)
    ffn_own = lax.psum_scatter(ffn_term, "attn", scatter_dimension=0, tiled=True)
    layer_out = (hidden_own + ffn_own.astype(jnp.float32)).astype(jnp.bfloat16)[None]
    return (layer_out, latent_out[None], rope_out[None])


def solution(mesh):
    placed = (
        P("expert", "attn", None),
        P("expert", None),
        P("expert", None, None),
        P("expert", None, None),
        P(),
        P(None, "attn"),
        P(),
        P(),
        P(None, "attn"),
        P(None, "attn"),
        P("attn", None),
        P(),
        P(),
        P("expert", None, "attn"),
        P("expert", None, "attn"),
        P("expert", "attn", None),
        P(None, "attn"),
        P(None, "attn"),
        P("attn", None),
    )
    return jax.shard_map(
        local,
        mesh=mesh,
        in_specs=placed,
        out_specs=(
            P("expert", "attn", None),
            P("expert", "attn", None, None),
            P("expert", "attn", None, None),
        ),
        check_vma=False,
    )
```

```python
import math

import jax
import jax.numpy as jnp
from jax import lax
from jax.sharding import PartitionSpec as P

NOPE = 128
ROPE = 64
VDIM = 128
LAT = 512
EXPERTS = 64
TOP = 6
PAGE = 128


epsilon = 1e-06


def rms_apply(values, gain_vec):
    mean_square = jnp.mean(values * values, axis=-1, keepdims=True)
    return values * lax.rsqrt(mean_square + epsilon) * gain_vec.astype(jnp.float32)


def rope_tables(positions, width_rope):
    half_width = width_rope // 2
    freq_index = jnp.arange(half_width, dtype=jnp.float32)
    inverse_freq = jnp.exp(freq_index * (-2.0 * math.log(10000.0) / width_rope))
    angles = positions.astype(jnp.float32)[:, None] * inverse_freq[None, :]
    return (jnp.cos(angles), jnp.sin(angles))


def rope_apply(values, cosine, sine):
    half_width = values.shape[-1] // 2
    first_half = values[..., :half_width]
    second_half = values[..., half_width:]
    return jnp.concatenate(
        [first_half * cosine - second_half * sine, second_half * cosine + first_half * sine],
        axis=-1,
    )


def write_pages(latent, key_rope, seg_lengths, starts, table, slot_ids, page_len):
    seg_count = table.shape[0]
    pages_per = table.shape[1]
    match = table[None, :, :] == slot_ids[:, None, None]
    seg_pick = jnp.sum(
        jnp.where(match, jnp.arange(seg_count, dtype=jnp.int32)[None, :, None], 0), axis=(1, 2)
    )
    page_pick = jnp.sum(
        jnp.where(match, jnp.arange(pages_per, dtype=jnp.int32)[None, None, :], 0), axis=(1, 2)
    )
    seg_match = seg_pick[:, None] == jnp.arange(seg_count, dtype=jnp.int32)[None, :]
    first_row = jnp.sum(jnp.where(seg_match, starts[None, :], 0), axis=1)
    seg_len = jnp.sum(jnp.where(seg_match, seg_lengths[None, :], 0), axis=1)
    offsets = page_pick[:, None] * page_len + jnp.arange(page_len, dtype=jnp.int32)[None, :]
    valid = offsets < seg_len[:, None]
    row_index = jnp.minimum(first_row[:, None] + offsets, latent.shape[0] - 1)
    latent_rows = jnp.take(latent, row_index, axis=0)
    rope_rows = jnp.take(key_rope, row_index, axis=0)
    zero_value = jnp.zeros((), latent.dtype)
    latent_out = jnp.where(valid[:, :, None], latent_rows, zero_value)
    rope_out = jnp.where(valid[:, None, :], jnp.transpose(rope_rows, (0, 2, 1)), zero_value)
    return (latent_out, rope_out)


def pick_matrix(routes_all, first_expert, local_experts, capacity):
    ids = first_expert + jnp.arange(local_experts, dtype=jnp.int32)
    hits = jnp.any(routes_all[:, None, :, :] == ids[None, :, None, None], axis=3)
    row_ids = jnp.arange(hits.shape[2], dtype=jnp.int32)
    earlier = (row_ids[:, None] < row_ids[None, :]).astype(jnp.bfloat16)
    before = jnp.einsum(
        "gek,kr->ger", hits.astype(jnp.bfloat16), earlier, preferred_element_type=jnp.float32
    ).astype(jnp.int32)
    slots = jnp.where(hits, before, -1)
    wanted = jnp.arange(capacity, dtype=jnp.int32)
    return (slots[:, :, None, :] == wanted[None, None, :, None]).astype(jnp.bfloat16)


def local(
    tokens,
    lengths,
    page_table,
    routes,
    attn_gain,
    w_query,
    w_latent,
    latent_gain,
    w_key,
    w_value,
    w_out,
    ffn_gain,
    w_router,
    expert_gate,
    expert_up,
    expert_down,
    shared_gate,
    shared_up,
    shared_down,
):
    quarters = lax.axis_size("attn")
    rank_attn = lax.axis_index("attn")
    owners = lax.axis_size("expert")
    own_rows = tokens.shape[1]
    group_rows = own_rows * quarters
    heads_here = w_value.shape[1] // VDIM
    local_experts = expert_gate.shape[0]
    capacity = quarters * (
        (7 * group_rows * TOP + 6 * EXPERTS * quarters - 1) // (6 * EXPERTS * quarters)
    )
    score_scale = (NOPE + ROPE) ** (-0.5)
    routes_all = lax.all_gather(routes[0], "expert", axis=0)
    first_expert = lax.axis_index("expert") * local_experts
    residual_own = tokens[0].astype(jnp.float32)
    normed_own = rms_apply(residual_own, attn_gain).astype(jnp.bfloat16)
    piece = lax.all_gather(normed_own, "attn", axis=0, tiled=True)
    projected = jnp.concatenate(
        [
            jnp.dot(piece, w_query, preferred_element_type=jnp.float32),
            jnp.dot(piece, w_latent, preferred_element_type=jnp.float32),
        ],
        axis=1,
    )
    seg_lengths = lengths[0]
    seg_ids = jnp.arange(seg_lengths.shape[0], dtype=jnp.int32)
    ends = jnp.sum(
        jnp.where(seg_ids[None, :] <= seg_ids[:, None], seg_lengths[None, :], 0), axis=1
    )
    starts = ends - seg_lengths
    row_ids = jnp.arange(group_rows, dtype=jnp.int32)
    seg_of_row = jnp.sum((row_ids[:, None] >= ends[None, :]).astype(jnp.int32), axis=1)
    seg_match = seg_of_row[:, None] == jnp.arange(seg_lengths.shape[0], dtype=jnp.int32)[None, :]
    positions = row_ids - jnp.sum(jnp.where(seg_match, starts[None, :], 0), axis=1)
    cosine, sine = rope_tables(positions, ROPE)
    query_width = w_query.shape[1]
    query_raw = projected[:, :query_width].reshape(group_rows, heads_here, NOPE + ROPE)
    query_all = jnp.concatenate(
        [
            query_raw[..., :NOPE],
            rope_apply(query_raw[..., NOPE:], cosine[:, None, :], sine[:, None, :]),
        ],
        axis=-1,
    ).astype(jnp.bfloat16)
    compressed = projected[:, query_width:]
    latent = rms_apply(compressed[:, :LAT], latent_gain).astype(jnp.bfloat16)
    key_rope = rope_apply(compressed[:, LAT:], cosine, sine).astype(jnp.bfloat16)
    key_nope = (
        jnp.dot(latent, w_key, preferred_element_type=jnp.float32)
        .astype(jnp.bfloat16)
        .reshape(group_rows, heads_here, NOPE)
    )
    value_rows = (
        jnp.dot(latent, w_value, preferred_element_type=jnp.float32)
        .astype(jnp.bfloat16)
        .reshape(group_rows, heads_here, VDIM)
    )
    slots_here = page_table.shape[1] * page_table.shape[2] // quarters
    slot_ids = rank_attn * slots_here + jnp.arange(slots_here, dtype=jnp.int32)
    latent_out, rope_out = write_pages(
        latent, key_rope, seg_lengths, starts, page_table[0], slot_ids, PAGE
    )
    query_ids = jnp.arange(group_rows, dtype=jnp.int32)
    score_nope = jnp.einsum(
        "qhd,khd->hqk", query_all[..., :NOPE], key_nope, preferred_element_type=jnp.float32
    )
    score_rope = jnp.einsum(
        "qhd,kd->hqk", query_all[..., NOPE:], key_rope, preferred_element_type=jnp.float32
    )
    scores = (score_nope + score_rope) * score_scale
    allowed = (seg_of_row[:, None] == seg_of_row[None, :]) & (
        row_ids[None, :] <= query_ids[:, None]
    )
    weights = jnp.where(allowed[None, :, :], jnp.exp(scores), 0.0)
    probs = (weights / jnp.sum(weights, axis=-1, keepdims=True)).astype(jnp.bfloat16)
    mixed = (
        jnp.einsum("hqk,khd->qhd", probs, value_rows, preferred_element_type=jnp.float32)
        .astype(jnp.bfloat16)
        .reshape(group_rows, heads_here * VDIM)
    )
    term_all = jnp.dot(mixed, w_out, preferred_element_type=jnp.float32)
    attn_own = lax.psum_scatter(
        term_all.astype(jnp.bfloat16), "attn", scatter_dimension=0, tiled=True
    ).astype(jnp.float32)
    hidden_own = residual_own + attn_own
    normed_ffn = rms_apply(hidden_own, ffn_gain).astype(jnp.bfloat16)
    width = normed_ffn.shape[1]
    rows_all = lax.all_gather(normed_ffn, ("expert", "attn"), axis=0, tiled=True).reshape(
        owners, group_rows, width
    )
    own_group = lax.axis_index("expert")
    normed_all = lax.dynamic_index_in_dim(rows_all, own_group, 0, keepdims=False)

    picks = pick_matrix(routes_all, first_expert, local_experts, capacity)

    logits = jnp.einsum("grd,dx->grx", rows_all, w_router, preferred_element_type=jnp.float32)
    exp_logits = jnp.exp(logits)
    router = exp_logits / jnp.sum(exp_logits, axis=-1, keepdims=True)
    router_here = lax.dynamic_slice_in_dim(router, first_expert, local_experts, 2)
    here = jnp.transpose(router_here, (2, 0, 1))
    slot_weight = jnp.sum(
        jnp.where(jnp.transpose(picks, (1, 0, 2, 3)) > 0, here[:, :, None, :], 0.0), axis=3
    ).reshape(local_experts, owners * capacity, 1)
    arrived = (
        jnp.einsum("gesr,grd->egsd", picks, rows_all, preferred_element_type=jnp.float32)
        .astype(jnp.bfloat16)
        .reshape(local_experts, owners * capacity, width)
    )
    gate_act = jnp.einsum("ech,ehf->ecf", arrived, expert_gate, preferred_element_type=jnp.float32)
    up_act = jnp.einsum("ech,ehf->ecf", arrived, expert_up, preferred_element_type=jnp.float32)
    hidden_act = (jax.nn.silu(gate_act) * up_act * slot_weight).astype(jnp.bfloat16)
    worked = (
        jnp.einsum("ecf,efh->ech", hidden_act, expert_down, preferred_element_type=jnp.float32)
        .astype(jnp.bfloat16)
        .reshape(local_experts, owners, capacity, width)
    )
    shared_hidden = (
        jax.nn.silu(jnp.dot(normed_all, shared_gate, preferred_element_type=jnp.float32))
        * jnp.dot(normed_all, shared_up, preferred_element_type=jnp.float32)
    ).astype(jnp.bfloat16)
    shared_term = jnp.dot(shared_hidden, shared_down, preferred_element_type=jnp.float32)
    group_ids = jnp.arange(owners, dtype=jnp.int32)[:, None, None]
    partial = (
        jnp.einsum("gesr,egsd->grd", picks, worked, preferred_element_type=jnp.float32)
        + jnp.where(group_ids == own_group, shared_term[None], 0.0)
    ).astype(jnp.bfloat16)
    ffn_own = lax.psum_scatter(
        partial.reshape(owners * group_rows, width),
        ("expert", "attn"),
        scatter_dimension=0,
        tiled=True,
    )
    layer_out = (hidden_own + ffn_own.astype(jnp.float32)).astype(jnp.bfloat16)[None]
    return (layer_out, latent_out[None], rope_out[None])


def solution(mesh):
    placed = (
        P("expert", "attn", None),
        P("expert", None),
        P("expert", None, None),
        P("expert", None, None),
        P(),
        P(None, "attn"),
        P(),
        P(),
        P(None, "attn"),
        P(None, "attn"),
        P("attn", None),
        P(),
        P(),
        P("expert", None, "attn"),
        P("expert", None, "attn"),
        P("expert", "attn", None),
        P(None, "attn"),
        P(None, "attn"),
        P("attn", None),
    )
    return jax.shard_map(
        local,
        mesh=mesh,
        in_specs=placed,
        out_specs=(
            P("expert", "attn", None),
            P("expert", "attn", None, None),
            P("expert", "attn", None, None),
        ),
        check_vma=False,
    )
```

```python
import math

import jax
import jax.numpy as jnp
from jax import lax
from jax.sharding import PartitionSpec as P

NOPE = 128
ROPE = 64
VDIM = 128
LAT = 512
EXPERTS = 64
TOP = 6
PAGE = 128


epsilon = 1e-06


def rms_apply(values, gain_vec):
    mean_square = jnp.mean(values * values, axis=-1, keepdims=True)
    return values * lax.rsqrt(mean_square + epsilon) * gain_vec.astype(jnp.float32)


def rope_tables(positions, width_rope):
    half_width = width_rope // 2
    freq_index = jnp.arange(half_width, dtype=jnp.float32)
    inverse_freq = jnp.exp(freq_index * (-2.0 * math.log(10000.0) / width_rope))
    angles = positions.astype(jnp.float32)[:, None] * inverse_freq[None, :]
    return (jnp.cos(angles), jnp.sin(angles))


def rope_apply(values, cosine, sine):
    half_width = values.shape[-1] // 2
    first_half = values[..., :half_width]
    second_half = values[..., half_width:]
    return jnp.concatenate(
        [first_half * cosine - second_half * sine, second_half * cosine + first_half * sine],
        axis=-1,
    )


def write_pages(latent, key_rope, seg_lengths, starts, table, slot_ids, page_len):
    seg_count = table.shape[0]
    pages_per = table.shape[1]
    match = table[None, :, :] == slot_ids[:, None, None]
    seg_pick = jnp.sum(
        jnp.where(match, jnp.arange(seg_count, dtype=jnp.int32)[None, :, None], 0), axis=(1, 2)
    )
    page_pick = jnp.sum(
        jnp.where(match, jnp.arange(pages_per, dtype=jnp.int32)[None, None, :], 0), axis=(1, 2)
    )
    seg_match = seg_pick[:, None] == jnp.arange(seg_count, dtype=jnp.int32)[None, :]
    first_row = jnp.sum(jnp.where(seg_match, starts[None, :], 0), axis=1)
    seg_len = jnp.sum(jnp.where(seg_match, seg_lengths[None, :], 0), axis=1)
    offsets = page_pick[:, None] * page_len + jnp.arange(page_len, dtype=jnp.int32)[None, :]
    valid = offsets < seg_len[:, None]
    row_index = jnp.minimum(first_row[:, None] + offsets, latent.shape[0] - 1)
    latent_rows = jnp.take(latent, row_index, axis=0)
    rope_rows = jnp.take(key_rope, row_index, axis=0)
    zero_value = jnp.zeros((), latent.dtype)
    latent_out = jnp.where(valid[:, :, None], latent_rows, zero_value)
    rope_out = jnp.where(valid[:, None, :], jnp.transpose(rope_rows, (0, 2, 1)), zero_value)
    return (latent_out, rope_out)


def pick_matrix(routes_all, first_expert, local_experts, capacity):
    ids = first_expert + jnp.arange(local_experts, dtype=jnp.int32)
    hits = jnp.any(routes_all[:, None, :, :] == ids[None, :, None, None], axis=3)
    row_ids = jnp.arange(hits.shape[2], dtype=jnp.int32)
    earlier = (row_ids[:, None] < row_ids[None, :]).astype(jnp.bfloat16)
    before = jnp.einsum(
        "gek,kr->ger", hits.astype(jnp.bfloat16), earlier, preferred_element_type=jnp.float32
    ).astype(jnp.int32)
    slots = jnp.where(hits, before, -1)
    wanted = jnp.arange(capacity, dtype=jnp.int32)
    return (slots[:, :, None, :] == wanted[None, None, :, None]).astype(jnp.bfloat16)


def local(
    tokens,
    lengths,
    page_table,
    routes,
    attn_gain,
    w_query,
    w_latent,
    latent_gain,
    w_key,
    w_value,
    w_out,
    ffn_gain,
    w_router,
    expert_gate,
    expert_up,
    expert_down,
    shared_gate,
    shared_up,
    shared_down,
):
    quarters = lax.axis_size("attn")
    rank_attn = lax.axis_index("attn")
    owners = lax.axis_size("expert")
    own_rows = tokens.shape[1]
    group_rows = own_rows * quarters
    heads_here = w_value.shape[1] // VDIM
    local_experts = expert_gate.shape[0]
    capacity = quarters * (
        (7 * group_rows * TOP + 6 * EXPERTS * quarters - 1) // (6 * EXPERTS * quarters)
    )
    score_scale = (NOPE + ROPE) ** (-0.5)
    routes_all = lax.all_gather(routes[0], "expert", axis=0)
    first_expert = lax.axis_index("expert") * local_experts
    residual_own = tokens[0].astype(jnp.float32)
    normed_own = rms_apply(residual_own, attn_gain).astype(jnp.bfloat16)
    piece = lax.all_gather(normed_own, "attn", axis=0, tiled=True)
    projected = jnp.concatenate(
        [
            jnp.dot(piece, w_query, preferred_element_type=jnp.float32),
            jnp.dot(piece, w_latent, preferred_element_type=jnp.float32),
        ],
        axis=1,
    )
    seg_lengths = lengths[0]
    seg_ids = jnp.arange(seg_lengths.shape[0], dtype=jnp.int32)
    ends = jnp.sum(
        jnp.where(seg_ids[None, :] <= seg_ids[:, None], seg_lengths[None, :], 0), axis=1
    )
    starts = ends - seg_lengths
    row_ids = jnp.arange(group_rows, dtype=jnp.int32)
    seg_of_row = jnp.sum((row_ids[:, None] >= ends[None, :]).astype(jnp.int32), axis=1)
    seg_match = seg_of_row[:, None] == jnp.arange(seg_lengths.shape[0], dtype=jnp.int32)[None, :]
    positions = row_ids - jnp.sum(jnp.where(seg_match, starts[None, :], 0), axis=1)
    cosine, sine = rope_tables(positions, ROPE)
    query_width = w_query.shape[1]
    query_raw = projected[:, :query_width].reshape(group_rows, heads_here, NOPE + ROPE)
    query_all = jnp.concatenate(
        [
            query_raw[..., :NOPE],
            rope_apply(query_raw[..., NOPE:], cosine[:, None, :], sine[:, None, :]),
        ],
        axis=-1,
    ).astype(jnp.bfloat16)
    compressed = projected[:, query_width:]
    latent = rms_apply(compressed[:, :LAT], latent_gain).astype(jnp.bfloat16)
    key_rope = rope_apply(compressed[:, LAT:], cosine, sine).astype(jnp.bfloat16)
    key_nope = (
        jnp.dot(latent, w_key, preferred_element_type=jnp.float32)
        .astype(jnp.bfloat16)
        .reshape(group_rows, heads_here, NOPE)
    )
    value_rows = (
        jnp.dot(latent, w_value, preferred_element_type=jnp.float32)
        .astype(jnp.bfloat16)
        .reshape(group_rows, heads_here, VDIM)
    )
    slots_here = page_table.shape[1] * page_table.shape[2] // quarters
    slot_ids = rank_attn * slots_here + jnp.arange(slots_here, dtype=jnp.int32)
    latent_out, rope_out = write_pages(
        latent, key_rope, seg_lengths, starts, page_table[0], slot_ids, PAGE
    )
    query_ids = jnp.arange(group_rows, dtype=jnp.int32)
    score_nope = jnp.einsum(
        "qhd,khd->hqk", query_all[..., :NOPE], key_nope, preferred_element_type=jnp.float32
    )
    score_rope = jnp.einsum(
        "qhd,kd->hqk", query_all[..., NOPE:], key_rope, preferred_element_type=jnp.float32
    )
    scores = (score_nope + score_rope) * score_scale
    allowed = (seg_of_row[:, None] == seg_of_row[None, :]) & (
        row_ids[None, :] <= query_ids[:, None]
    )
    weights = jnp.where(allowed[None, :, :], jnp.exp(scores), 0.0)
    probs = (weights / jnp.sum(weights, axis=-1, keepdims=True)).astype(jnp.bfloat16)
    mixed = (
        jnp.einsum("hqk,khd->qhd", probs, value_rows, preferred_element_type=jnp.float32)
        .astype(jnp.bfloat16)
        .reshape(group_rows, heads_here * VDIM)
    )
    term_all = jnp.dot(mixed, w_out, preferred_element_type=jnp.float32)
    attn_own = lax.psum_scatter(
        term_all.astype(jnp.bfloat16), "attn", scatter_dimension=0, tiled=True
    ).astype(jnp.float32)
    hidden_own = residual_own + attn_own
    normed_ffn = rms_apply(hidden_own, ffn_gain).astype(jnp.bfloat16)
    width = normed_ffn.shape[1]
    rows_all = lax.all_gather(normed_ffn, ("expert", "attn"), axis=0, tiled=True).reshape(
        owners, group_rows, width
    )
    own_group = lax.axis_index("expert")
    normed_all = lax.dynamic_index_in_dim(rows_all, own_group, 0, keepdims=False)

    picks = pick_matrix(routes_all, first_expert, local_experts, capacity)

    logits = jnp.einsum("grd,dx->grx", rows_all, w_router, preferred_element_type=jnp.float32)
    exp_logits = jnp.exp(logits)
    router = exp_logits / jnp.sum(exp_logits, axis=-1, keepdims=True)
    router_here = lax.dynamic_slice_in_dim(router, first_expert, local_experts, 2)
    here = jnp.transpose(router_here, (2, 0, 1))
    slot_weight = jnp.sum(
        jnp.where(jnp.transpose(picks, (1, 0, 2, 3)) > 0, here[:, :, None, :], 0.0), axis=3
    ).reshape(local_experts, owners * capacity, 1)
    arrived = (
        jnp.einsum("gesr,grd->egsd", picks, rows_all, preferred_element_type=jnp.float32)
        .astype(jnp.bfloat16)
        .reshape(local_experts, owners * capacity, width)
    )
    gate_act = jnp.einsum("ech,ehf->ecf", arrived, expert_gate, preferred_element_type=jnp.float32)
    up_act = jnp.einsum("ech,ehf->ecf", arrived, expert_up, preferred_element_type=jnp.float32)
    hidden_act = (jax.nn.silu(gate_act) * up_act * slot_weight).astype(jnp.bfloat16)
    worked = (
        jnp.einsum("ecf,efh->ech", hidden_act, expert_down, preferred_element_type=jnp.float32)
        .astype(jnp.bfloat16)
        .reshape(local_experts, owners, capacity, width)
    )
    shared_hidden = (
        jax.nn.silu(jnp.dot(normed_all, shared_gate, preferred_element_type=jnp.float32))
        * jnp.dot(normed_all, shared_up, preferred_element_type=jnp.float32)
    ).astype(jnp.bfloat16)
    shared_term = jnp.dot(shared_hidden, shared_down, preferred_element_type=jnp.float32)
    partial = jnp.einsum(
        "gesr,egsd->grd", picks, worked, preferred_element_type=jnp.float32
    ).astype(jnp.bfloat16)
    group_sum = lax.psum_scatter(partial, "expert", scatter_dimension=0, tiled=False)
    ffn_term = (group_sum.astype(jnp.float32) + shared_term).astype(jnp.bfloat16)
    ffn_own = lax.psum_scatter(ffn_term, "attn", scatter_dimension=0, tiled=True)
    layer_out = (hidden_own + ffn_own.astype(jnp.float32)).astype(jnp.bfloat16)[None]
    return (layer_out, latent_out[None], rope_out[None])


def solution(mesh):
    placed = (
        P("expert", "attn", None),
        P("expert", None),
        P("expert", None, None),
        P("expert", None, None),
        P(),
        P(None, "attn"),
        P(),
        P(),
        P(None, "attn"),
        P(None, "attn"),
        P("attn", None),
        P(),
        P(),
        P("expert", None, "attn"),
        P("expert", None, "attn"),
        P("expert", "attn", None),
        P(None, "attn"),
        P(None, "attn"),
        P("attn", None),
    )
    return jax.shard_map(
        local,
        mesh=mesh,
        in_specs=placed,
        out_specs=(
            P("expert", "attn", None),
            P("expert", "attn", None, None),
            P("expert", "attn", None, None),
        ),
        check_vma=False,
    )
```
